256 devices in a mesh: tp: 4 (over y), ep: 64 (over z, x, core).
Axes of the slice: x: 4, y: 4, z: 8, core: 2. Of those that a mesh axis runs over, the one named last changes fastest.
Arguments:
- grad_out: bfloat16 [8192, 5120], P('ep', 'tp'), may hold values from -1.5 to 1.5
- routes: int32 [8192, 6], P('ep'), may hold values from 0 to 63, all different within a row; in each aligned block of 128 rows (0 to 127, 128 to 255, ...) at most 24 rows name the same one
- gates: float32 [8192, 6], P('ep'), may hold values from 0.03 to 0.6
- saved_gate: bfloat16 [64, 64, 24, 1536], P('ep', None, None, 'tp'), may hold values from -6 to 6
- saved_up: bfloat16 [64, 64, 24, 1536], P('ep', None, None, 'tp'), may hold values from -6 to 6
- w_down: bfloat16 [64, 1536, 5120], P('ep', 'tp'), may hold values from -0.15625 to 0.15625
Outputs:
- grad_gate: bfloat16 [64, 64, 24, 1536], P('ep', None, None, 'tp')
- grad_up: bfloat16 [64, 64, 24, 1536], P('ep', None, None, 'tp')
- grad_w_down: bfloat16 [64, 1536, 5120], P('ep', 'tp')
- grad_gates: float32 [8192, 6], P('ep')
The draws below stay inside these ranges and needn't reach their ends.
Inputs may be any that keep to these rules, and one draw needn't show every extreme that they name: `routes`: the 6 ids of a row differ. In each aligned block of 128 rows (the tokens of one index of ep) no id is named by more than 24 rows, and some id reaches 24 in some block; every id is named somewhere.
All inputs are finite; a program needn't handle non-finite values.
Results may differ from the reference program's by a relative error of at most 0.007.
Values may be sent and summed in bfloat16 or wider, within the bound.
A program may use at most 128 MiB of HBM per device.

```python
import math
import jax
import jax.numpy as jnp
import numpy as np
from jax import lax

D = 5120
FF = 1536
TOP = 6
TOK_DEV = 128
EXPERTS = 64
SOURCES = 64
CAP = 24
TOKENS = 8192
N_EP = 64


def block_scale(key, dims, split, low, largest):
    loudness = 1.0
    for position, blocks in split:
        draws = jax.random.uniform(jax.random.fold_in(jax.random.fold_in(key, 6), position), (blocks,), jnp.float32, low / len(split), largest / len(split))
        loudness = loudness * jnp.repeat(jnp.exp(draws), dims[position] // blocks).reshape((-1,) + (1,) * (len(dims) - 1 - position))
    return loudness


def assign_block(stream_key, own, number, rows, number_of, top, most, lean):
    sequence = jax.random.permutation(stream_key, number_of)
    crowded, ordinary = load_shares(number_of, rows * top, most, lean, True), load_shares(number_of, rows * top, most, lean, False)
    places = jnp.arange(number_of)

    def named(lengths, rotation):
        used = int((lengths > 0).sum())
        fixed = max(1, used // 4)
        shifted = fixed + (places - fixed + rotation * (used - fixed)) % max(1, number_of - fixed)
        return jnp.zeros((number_of,), jnp.int32).at[sequence[jnp.where(places < fixed, places, shifted)]].set(jnp.asarray(lengths, jnp.int32))

    lengths = jnp.where(number % 4 == 0, named(crowded, number // 4), named(ordinary, number - number // 4 - 1))
    mixed = jax.random.permutation(jax.random.fold_in(own, 3), number_of)
    source_of, taker = mixed[0:number_of // 2 * 2:2], mixed[1:number_of // 2 * 2:2]
    margin = jnp.minimum(lengths[source_of] - 1, most - lengths[taker]) // 2
    margin = jnp.where((source_of == sequence[0]) | (taker == sequence[0]) | (lengths[taker] == 0), 0, jnp.maximum(margin, 0))
    shifted = jax.random.randint(jax.random.fold_in(own, 4), (number_of // 2,), 0, 1 << 20) % (margin + 1)
    lengths = lengths.at[source_of].add(-shifted).at[taker].add(shifted)
    members = jnp.searchsorted(jnp.cumsum(lengths), jnp.arange(rows * top), side="right").astype(jnp.int32)
    listing = members.reshape(top, rows).T
    listing = listing[jax.random.permutation(jax.random.fold_in(own, 1), rows)]
    rotation = jax.random.randint(jax.random.fold_in(own, 2), (rows, 1), 0, top)
    return jnp.take_along_axis(listing, (jnp.arange(top)[None, :] + rotation) % top, axis=1)


def load_shares(amount, total, bound, lean, full):
    portions = [(1 << 20) // math.isqrt(rank ** lean) + 1 for rank in range(1, amount + 1)]
    largest = bound if full else min(bound, max(-(-total // amount), total * portions[0] // sum(portions)))
    least = 1 if total - largest >= amount - 1 else 0
    given, spare = [largest] + [least] * (amount - 1), total - largest - least * (amount - 1)
    while spare > 0:
        candidates = [i for i in range(1, amount) if given[i] < largest] or [i for i in range(1, amount) if given[i] < bound]
        pool, budget = sum([portions[i] for i in candidates]), spare
        for i in candidates:
            more = min(bound - given[i], max(1, budget * portions[i] // pool), spare)
            given[i] = given[i] + more
            spare = spare - more
    return np.array(given)


def bell_draw(rng, shape, width, bound, pieces=(), kind=jnp.bfloat16):
    entries = width * jax.random.normal(rng, shape, jnp.float32)
    if pieces:
        entries = entries * block_scale(rng, shape, pieces, -0.22, 0.18)
    return jnp.clip(entries, -bound, bound).astype(kind)


def setup_inputs(seed: int = 0) -> dict:
    seeds = jax.random.split(jax.random.key(seed), 7)
    grad_out = bell_draw(seeds[0], (TOKENS, D), 0.25, 1.5, ((0, 64), (1, 4)))
    routes_keys = jax.random.split(jax.random.fold_in(seeds[1], 1), TOKENS // TOK_DEV)
    routes_turns = jax.random.permutation(jax.random.fold_in(seeds[1], 3), TOKENS // TOK_DEV)
    routes = jax.vmap(lambda own, number: assign_block(jax.random.fold_in(seeds[1], 2), own, number, TOK_DEV, EXPERTS, TOP, CAP, 2))(routes_keys, routes_turns).reshape((TOKENS, TOP))
    gates = jnp.clip(jnp.exp(math.log(0.6) - 2.9957323 * jax.random.uniform(seeds[2], (TOKENS, TOP), jnp.float32) ** block_scale(seeds[2], (TOKENS, TOP), ((0, 64),), -0.2, 0.2)), 0.03, 0.6)
    saved_gate = bell_draw(seeds[3], (EXPERTS, SOURCES, CAP, FF), 1.0, 6.0, ((0, 64), (3, 4)))
    saved_up = bell_draw(seeds[4], (EXPERTS, SOURCES, CAP, FF), 1.0, 6.0, ((0, 64), (3, 4)))
    w_down = bell_draw(seeds[5], (EXPERTS, FF, D), FF ** -0.5, 0.15625, ((0, 64), (1, 4)))
    return {"grad_out": grad_out, "routes": routes, "gates": gates, "saved_gate": saved_gate, "saved_up": saved_up, "w_down": w_down}


def slot_numbers(routes):
    flat_routes = routes.reshape(N_EP, TOK_DEV * TOP)
    onehot = (flat_routes[:, :, None] == jnp.arange(EXPERTS, dtype=jnp.int32)[None, None, :]).astype(jnp.int32)
    earlier = jnp.cumsum(onehot, axis=1) - onehot
    return jnp.sum(earlier * onehot, axis=2).astype(jnp.int32).reshape(TOKENS, TOP)


def reference(grad_out, routes, gates, saved_gate, saved_up, w_down):
    slot_ids = slot_numbers(routes)
    source = (jnp.arange(TOKENS, dtype=jnp.int32) // TOK_DEV).astype(jnp.int32)
    slot_count = SOURCES * CAP

    def per_expert(expert):
        hit = routes == expert
        present = jnp.any(hit, axis=1)
        slot_tok = jnp.sum(jnp.where(hit, slot_ids, 0), axis=1).astype(jnp.int32)
        prob_tok = jnp.sum(jnp.where(hit, gates, jnp.float32(0.0)), axis=1)
        index = jnp.where(present, source * CAP + slot_tok, slot_count).astype(jnp.int32)
        routed = jnp.zeros((slot_count, D), jnp.bfloat16).at[index].set(grad_out, mode="drop")
        slot_prob = jnp.zeros((slot_count,), jnp.float32).at[index].set(prob_tok, mode="drop")[:, None]
        gate_vals = saved_gate[expert].reshape(slot_count, FF).astype(jnp.float32)
        up_vals = saved_up[expert].reshape(slot_count, FF).astype(jnp.float32)
        weight = w_down[expert]
        grad_hidden = jnp.dot(routed, weight.T, preferred_element_type=jnp.float32)
        sigmoid = jax.nn.sigmoid(gate_vals)
        activation = gate_vals * sigmoid
        hidden = (activation * up_vals).astype(jnp.bfloat16)
        slot_grad = jnp.sum(hidden.astype(jnp.float32) * grad_hidden, axis=1)
        scaled_hidden = slot_prob * grad_hidden
        slope = sigmoid * (1.0 + gate_vals * (1.0 - sigmoid))
        grad_gate = (scaled_hidden * up_vals * slope).astype(jnp.bfloat16).reshape(SOURCES, CAP, FF)
        grad_up = (scaled_hidden * activation).astype(jnp.bfloat16).reshape(SOURCES, CAP, FF)
        scaled = (slot_prob * routed.astype(jnp.float32)).astype(jnp.bfloat16)
        grad_weight = jnp.dot(hidden.T, scaled, preferred_element_type=jnp.float32).astype(jnp.bfloat16)
        padded = jnp.concatenate([slot_grad, jnp.zeros((1,), jnp.float32)])
        value = padded[index]
        contribution = jnp.where(hit, value[:, None], jnp.float32(0.0))
        return grad_gate, grad_up, grad_weight, contribution

    grad_gate, grad_up, grad_w_down, contributions = lax.map(per_expert, jnp.arange(EXPERTS, dtype=jnp.int32))
    grad_gates = jnp.sum(contributions, axis=0)
    return grad_gate, grad_up, grad_w_down, grad_gates
```

```python
import functools

import jax
import jax.numpy as jnp
from jax import lax
from jax.experimental import pallas as pl
from jax.experimental.pallas import tpu as pltpu
from jax.sharding import PartitionSpec as P

NZ, NX, NY = 8, 4, 4
CAP = 24
TOK = 128
TOP = 6
EXTRA = 256
META = 128
SLAB = 2 * CAP
ROWS = NX * SLAB
PARTNER_SLOT = (0, 2, 1, 4, 3, 6, 5, 7)
OFFSETS = (0, -1, 1, -2, 2, -3, 3, -4)
F32 = jnp.float32
BF16 = jnp.bfloat16
MESH = pl.DeviceIdType.MESH


def chunks(total, size):
    return [(at, min(size, total - at)) for at in range(0, total, size)]


def kernel(
    feats,
    width,
    tok_ref,
    meta_ref,
    gate_hbm,
    up_hbm,
    w_hbm,
    gg_ref,
    gu_ref,
    gw_ref,
    sl_ref,
    tok,
    pk,
    rx,
    ro,
    ry,
    w,
    sg,
    su,
    hs,
    hst,
    in_sem,
    e_send,
    e_recv,
    z_send,
    z_recv,
    c_send,
    c_recv,
    x_send,
    x_recv,
    y_send,
    y_recv,
):
    y = lax.axis_index("tp")
    ep = lax.axis_index("ep")
    z = ep // 8
    x = (ep // 2) % 4
    c = ep % 2
    d = 1 - 2 * c
    main = feats - EXTRA

    def ep_at(zz, xx, cc):
        return {"ep": zz * 8 + xx * 2 + cc}

    z_fwd, z_bwd = ep_at((z + d + 8) % 8, x, c), ep_at((z - d + 8) % 8, x, c)
    x_fwd, x_bwd = ep_at(z, (x + d + 4) % 4, c), ep_at(z, (x - d + 4) % 4, c)
    y_fwd, y_bwd = {"tp": (y + d + 4) % 4}, {"tp": (y - d + 4) % 4}
    partner = ep_at(z, x, 1 - c)

    barrier = pltpu.get_barrier_semaphore()
    for peer in (z_fwd, z_bwd, x_fwd, x_bwd, y_fwd, y_bwd, partner):
        pl.semaphore_signal(barrier, inc=1, device_id=peer, device_id_type=MESH)

    loads = [
        pltpu.make_async_copy(w_hbm, w, in_sem.at[0]),
        pltpu.make_async_copy(gate_hbm, sg, in_sem.at[1]),
        pltpu.make_async_copy(up_hbm, su, in_sem.at[2]),
    ]
    for load in loads:
        load.start()
    tok[0, 0:TOK, 0:feats] = tok_ref[...]
    tok[0, 0:TOK, width - META : width] = meta_ref[...]
    pl.semaphore_wait(barrier, 7)

    sends = []

    def remote(src, dst, send, recv, peer):
        return pltpu.make_async_remote_copy(
            src_ref=src,
            dst_ref=dst,
            send_sem=send,
            recv_sem=recv,
            device_id=peer,
            device_id_type=MESH,
        )

    def start(*args):
        copy = remote(*args)
        copy.start()
        sends.append(copy)

    def extra_at(slot):
        return tok.at[0, 0:TOK, pl.ds(pl.multiple_of(feats + slot * EXTRA, 128), EXTRA)]

    from_bwd, from_fwd = (3 - d) % 4, (3 + d) % 4
    mine = tok_ref.at[:, main:feats]
    start(mine, extra_at(from_bwd), e_send.at[0], e_recv.at[0], y_fwd)
    start(mine, extra_at(from_fwd), e_send.at[1], e_recv.at[1], y_bwd)
    remote(mine, extra_at(from_bwd), e_send.at[0], e_recv.at[0], y_bwd).wait_recv()
    start(extra_at(from_bwd), extra_at(1), e_send.at[2], e_recv.at[2], y_fwd)
    remote(mine, extra_at(from_fwd), e_send.at[1], e_recv.at[1], y_fwd).wait_recv()
    remote(mine, extra_at(1), e_send.at[2], e_recv.at[2], y_bwd).wait_recv()

    def own(j):
        return tok.at[j, 0:TOK]

    def other(j):
        return tok.at[j, TOK : 2 * TOK]

    def z_copy(src, dst, peer):
        return (own(src), own(dst), z_send.at[dst], z_recv.at[dst], peer)

    def row_ids(j, half, core):
        table = tok[j, half * TOK : (half + 1) * TOK, width - META : width].astype(F32).T
        expert = table[0:8].astype(jnp.int32) - 1
        slot = table[32:40].astype(jnp.int32)
        hit = (lax.shift_right_arithmetic(expert, 3) == z) & ((expert & 1) == c)
        relative = ((lax.shift_right_arithmetic(expert, 1) & 3) - x) * d & 3
        return jnp.where(hit, relative * SLAB + core * CAP + slot, -1)

    def one_hot(ids):
        rows = lax.broadcasted_iota(jnp.int32, (ROWS, TOK), 0)
        found = rows == ids[0:1]
        for k in range(1, TOP):
            found = found | (rows == ids[k : k + 1])
        return jnp.where(found, 1.0, 0.0).astype(BF16)

    def x_slab(j, xx):
        return ro.at[pl.ds(pl.multiple_of(j * ROWS + xx * SLAB, 16), SLAB)]

    def take_tokens(j):
        if j == 0:
            start(*z_copy(0, 1, z_fwd))
            start(*z_copy(0, 2, z_bwd))
        else:
            remote(*z_copy(j, j, z_fwd)).wait_recv()
            if j in (1, 3, 5):
                start(*z_copy(j, j + 2, z_fwd))
            elif j in (2, 4):
                start(*z_copy(j, j + 2, z_bwd))
        to = PARTNER_SLOT[j]
        start(own(j), other(to), c_send.at[to], c_recv.at[to], partner)

    def pack(j):
        remote(own(j), other(j), c_send.at[j], c_recv.at[j], partner).wait_recv()
        picker = jnp.concatenate([one_hot(row_ids(j, 0, c)), one_hot(row_ids(j, 1, 1 - c))], axis=1)
        here = pl.ds(pl.multiple_of(j * ROWS + x * SLAB, 16), SLAB)
        for at, size in chunks(width, 512):
            rows = jnp.dot(picker, tok[j, :, at : at + size], preferred_element_type=F32).astype(BF16)
            ro[here, at : at + size] = rows[0:SLAB]
            pk[j, :, at : at + size] = rows[SLAB:ROWS]
        start(pk.at[j, 0:SLAB], x_slab(j, x), x_send.at[j, 0], x_recv.at[j, 0], x_fwd)
        start(pk.at[j, SLAB : 2 * SLAB], rx.at[j], x_send.at[j, 2], x_recv.at[j, 2], x_fwd)
        start(pk.at[j, 2 * SLAB : 3 * SLAB], x_slab(j, x), x_send.at[j, 1], x_recv.at[j, 1], x_bwd)

    def x_relay(j):
        before = (x - d + 4) % 4
        remote(rx.at[j], rx.at[j], x_send.at[j, 2], x_recv.at[j, 2], x_bwd).wait_recv()
        start(rx.at[j], x_slab(j, before), x_send.at[j, 3], x_recv.at[j, 3], x_fwd)

    def y_block(i, j):
        return ry.at[i, j * ROWS : (j + 1) * ROWS]

    def send_y(j):
        for i, away in ((0, -d), (1, d), (3, 2)):
            slab = x_slab(j, (x + away + 4) % 4)
            remote(rx.at[j], slab, x_send.at[j, i], x_recv.at[j, i], x_bwd).wait_recv()
        block = ro.at[j * ROWS : (j + 1) * ROWS, 0:main]
        start(block, y_block(0, j), y_send.at[j, 0], y_recv.at[j, 0], y_fwd)
        start(block, y_block(1, j), y_send.at[j, 1], y_recv.at[j, 1], y_bwd)

    def y_relay(j):
        remote(y_block(0, j), y_block(0, j), y_send.at[j, 0], y_recv.at[j, 0], y_bwd).wait_recv()
        start(y_block(0, j), y_block(2, j), y_send.at[j, 2], y_recv.at[j, 2], y_fwd)

    def columns(at, size):
        return pl.ds(pl.multiple_of(at, 128), size)

    owners = ((y - d + 4) % 4, (y + d + 4) % 4, (y + 2) % 4)

    def compute(j):
        for i in (1, 2):
            remote(y_block(i, j), y_block(i, j), y_send.at[j, i], y_recv.at[j, i], y_bwd).wait_recv()
        if j == 0:
            for load in loads:
                load.wait()
        rows = slice(j * ROWS, (j + 1) * ROWS)

        def times(left, at, size):
            return lax.dot_general(
                left, w[:, columns(at, size)], (((1,), (1,)), ((), ())), preferred_element_type=F32
            )

        grad = times(ro[rows, 0:feats], y * feats, feats)
        for s in range(3):
            at = feats + s * EXTRA
            owner = (y + 1 + s) % 4
            grad += times(ro[rows, at : at + EXTRA], owner * feats + main, EXTRA)
        for i in range(3):
            grad += times(ry[i, rows, :], owners[i] * feats, main)

        meta = ro[rows, width - META : width].astype(F32)
        lanes = lax.broadcasted_iota(jnp.int32, (ROWS, META), 1)
        weight = (
            pltpu.roll(meta, META - 8, 1) + pltpu.roll(meta, META - 16, 1)
        ) + pltpu.roll(meta, META - 24, 1)
        chosen = (lanes < TOP) & (meta.astype(jnp.int32) == ep + 1)
        prob = jnp.sum(jnp.where(chosen, weight, 0.0), axis=1, keepdims=True)

        zz = (z + OFFSETS[j] * d + 8) % 8
        place = pl.ds(pl.multiple_of(zz * ROWS, 16), ROWS)
        gate = sg[place, :].astype(F32)
        up = su[place, :].astype(F32)
        sigmoid = jax.nn.sigmoid(gate)
        activation = gate * sigmoid
        product = activation * up
        rounded = product.astype(BF16).astype(F32)
        hs[rows, :] = (prob * product).astype(BF16)
        part = rounded * grad
        part = part[:, 0:128] + part[:, 128:256] + part[:, 256:384]
        sl_ref[pl.ds(zz, 1), :] = jnp.sum(part.T, axis=0, keepdims=True)
        scaled = prob * grad
        slope = sigmoid * (1.0 + gate * (1.0 - sigmoid))
        gg_ref[place, :] = (scaled * up * slope).astype(BF16)
        gu_ref[place, :] = (scaled * activation).astype(BF16)

    for step in range(8 + 3):
        if step < 8:
            for j in ((0,), (1, 2), (), (3, 4), (), (5, 6), (), (7,))[step]:
                take_tokens(j)
            pack(step)
        if 0 <= step - 1 < 8:
            x_relay(step - 1)
            send_y(step - 1)
        if 0 <= step - 2 < 8:
            y_relay(step - 2)
        if 0 <= step - 3 < 8:
            compute(step - 3)

    hst[...] = hs[...].T

    def weights(block, at, size):
        for piece, wide in chunks(size, 256):
            total = jnp.dot(
                hst[...], block(piece, wide), preferred_element_type=F32
            )
            gw_ref[:, columns(at + piece, wide)] = total.astype(BF16)

    weights(lambda at, size: ro[:, at : at + size], y * feats, feats)
    for s in range(3):
        owner = (y + 1 + s) % 4
        base = feats + s * EXTRA
        weights(lambda at, size: ro[:, base + at : base + at + size], owner * feats + main, EXTRA)
    for i in range(3):
        weights(lambda at, size: ry[i, :, at : at + size], owners[i] * feats, main)
    for copy in sends:
        copy.wait_send()


def slot_numbers(routes, experts):
    flat_routes = routes.reshape(-1)
    onehot = (flat_routes[:, None] == jnp.arange(experts, dtype=jnp.int32)[None, :]).astype(
        jnp.int32
    )
    earlier = jnp.cumsum(onehot, axis=0) - onehot
    return jnp.sum(earlier * onehot, axis=1).reshape(routes.shape)


def body(grad_out, routes, gates, saved_gate, saved_up, w_down):
    experts = lax.axis_size("ep")
    feats = grad_out.shape[1]
    hidden_units = saved_gate.shape[3]
    slots = experts * CAP
    width = feats + 3 * EXTRA + META
    slot_ids = slot_numbers(routes, experts)
    target = routes * CAP + slot_ids
    places = jnp.arange(slots, dtype=jnp.int32)
    matches = target[None, :, :] == places[:, None, None]

    high = lax.reduce_precision(gates, 8, 7)
    middle = lax.reduce_precision(gates - high, 8, 7)
    low = gates - high - middle
    parts = (routes.astype(F32) + 1.0, high, middle, low, slot_ids.astype(F32))
    meta = jnp.concatenate([jnp.pad(part, ((0, 0), (0, 8 - TOP))) for part in parts], axis=1)
    meta = jnp.pad(meta, ((0, 0), (0, META - 40))).astype(BF16)

    vmem = pl.BlockSpec(memory_space=pltpu.VMEM)
    hbm = pl.BlockSpec(memory_space=pl.ANY)
    dma = pltpu.SemaphoreType.DMA
    main = feats - EXTRA
    flops = 4 * slots * hidden_units * feats * NY
    grad_gate, grad_up, grad_w, slot_grad = pl.pallas_call(
        functools.partial(kernel, feats, width),
        out_shape=(
            jax.ShapeDtypeStruct((slots, hidden_units), BF16),
            jax.ShapeDtypeStruct((slots, hidden_units), BF16),
            jax.ShapeDtypeStruct((hidden_units, feats * NY), BF16),
            jax.ShapeDtypeStruct((NZ, ROWS), F32),
        ),
        in_specs=[vmem, vmem, hbm, hbm, hbm],
        out_specs=(vmem, vmem, vmem, vmem),
        scratch_shapes=[
            pltpu.VMEM((NZ, 2 * TOK, width), BF16),
            pltpu.VMEM((NZ, 3 * SLAB, width), BF16),
            pltpu.VMEM((NZ, SLAB, width), BF16),
            pltpu.VMEM((slots, width), BF16),
            pltpu.VMEM((3, slots, main), BF16),
            pltpu.VMEM((hidden_units, feats * NY), BF16),
            pltpu.VMEM((slots, hidden_units), BF16),
            pltpu.VMEM((slots, hidden_units), BF16),
            pltpu.VMEM((slots, hidden_units), BF16),
            pltpu.VMEM((hidden_units, slots), BF16),
            dma((3,)),
            dma((3,)),
            dma((3,)),
            dma((NZ,)),
            dma((NZ,)),
            dma((NZ,)),
            dma((NZ,)),
            dma((NZ, 4)),
            dma((NZ, 4)),
            dma((NZ, 3)),
            dma((NZ, 3)),
        ],
        compiler_params=pltpu.CompilerParams(
            collective_id=0, has_side_effects=True, vmem_limit_bytes=60 * 1024 * 1024
        ),
        cost_estimate=pl.CostEstimate(
            flops=flops, bytes_accessed=16 * 1024 * 1024, transcendentals=slots * hidden_units
        ),
    )(
        grad_out,
        meta,
        saved_gate.reshape(slots, hidden_units),
        saved_up.reshape(slots, hidden_units),
        w_down[0],
    )

    returned = lax.all_to_all(
        slot_grad.reshape(experts, CAP), "ep", split_axis=0, concat_axis=0, tiled=True
    )
    flat_back = returned.reshape(-1)
    picked = jnp.sum(jnp.where(matches, flat_back[:, None, None], jnp.float32(0.0)), axis=0)
    grad_gates = lax.psum(picked, "tp")
    return (
        grad_gate.reshape(saved_gate.shape),
        grad_up.reshape(saved_up.shape),
        grad_w[None],
        grad_gates,
    )


def solution(mesh):
    in_specs = (
        P("ep", "tp"),
        P("ep", None),
        P("ep", None),
        P("ep", None, None, "tp"),
        P("ep", None, None, "tp"),
        P("ep", "tp", None),
    )
    out_specs = (
        P("ep", None, None, "tp"),
        P("ep", None, None, "tp"),
        P("ep", "tp", None),
        P("ep", None),
    )
    return jax.shard_map(body, mesh=mesh, in_specs=in_specs, out_specs=out_specs, check_vma=False)
```

```python
import functools

import jax
import jax.numpy as jnp
from jax import lax
from jax.experimental import pallas as pl
from jax.experimental.pallas import tpu as pltpu
from jax.sharding import PartitionSpec as P

NZ, NX, NY = 8, 4, 4
CAP = 24
EXPERTS = 64
TOK = 128
TOP = 6
EXTRA = 384
META = 128
SLAB = 2 * CAP
ROWS = NX * SLAB
PARTNER_SLOT = (0, 2, 1, 4, 3, 6, 5, 7)
ORDER = (
    "T0 P0 Y0 T1 T2 P1 P2 Y1 R0 T3 T4 P3 Y2 R1 C0 P4 Y3 R2 C1 T5 T6 P5 Y4 R3 C2 "
    "P6 Y5 R4 C3 T7 P7 Y6 R5 C4 Y7 R6 C5 R7 C6 C7"
)
OFFSETS = (0, -1, 1, -2, 2, -3, 3, -4)
F32 = jnp.float32
BF16 = jnp.bfloat16
MESH = pl.DeviceIdType.MESH


def chunks(total, size):
    return [(at, min(size, total - at)) for at in range(0, total, size)]


def kernel(
    feats,
    width,
    tok_ref,
    routes_ref,
    gates_ref,
    gate_hbm,
    up_hbm,
    w_hbm,
    gg_ref,
    gu_ref,
    gw_ref,
    back_ref,
    tok,
    pk,
    ro,
    ry,
    w,
    sg,
    su,
    hs,
    hst,
    table,
    sl,
    sums,
    theirs,
    zs,
    zr,
    in_sem,
    e_send,
    e_recv,
    z_send,
    z_recv,
    c_send,
    c_recv,
    x_send,
    x_recv,
    y_send,
    y_recv,
    s_send,
    s_recv,
    b_send,
    b_recv,
):
    y = lax.axis_index("tp")
    ep = lax.axis_index("ep")
    z = ep // 8
    x = (ep // 2) % 4
    c = ep % 2
    d = 1 - 2 * c
    main = feats - EXTRA

    def ep_at(zz, xx, cc):
        return {"ep": zz * 8 + xx * 2 + cc}

    z_fwd, z_bwd = ep_at((z + d + 8) % 8, x, c), ep_at((z - d + 8) % 8, x, c)
    x_fwd, x_bwd = ep_at(z, (x + d + 4) % 4, c), ep_at(z, (x - d + 4) % 4, c)
    x_far = ep_at(z, (x + 2) % 4, c)
    y_far = {"tp": (y + 2) % 4}
    y_fwd, y_bwd = {"tp": (y + d + 4) % 4}, {"tp": (y - d + 4) % 4}
    partner = ep_at(z, x, 1 - c)

    barrier = pltpu.get_barrier_semaphore()
    z_far = [ep_at((z + o) % 8, x, c) for o in range(2, 7)]
    for peer in [z_fwd, z_bwd, x_fwd, x_far, x_bwd, y_fwd, y_far, y_bwd, partner] + z_far:
        pl.semaphore_signal(barrier, inc=1, device_id=peer, device_id_type=MESH)

    loads = [
        pltpu.make_async_copy(w_hbm, w, in_sem.at[0]),
        pltpu.make_async_copy(gate_hbm, sg, in_sem.at[1]),
        pltpu.make_async_copy(up_hbm, su, in_sem.at[2]),
    ]
    for load in loads:
        load.start()
    tok[0, 0:TOK, 0:feats] = tok_ref[...]
    table[...] = jnp.zeros((META, TOK), F32)
    table[0:TOP] = routes_ref[...].astype(F32) + 1.0
    gates = gates_ref[...]
    high = gates.astype(BF16).astype(F32)
    middle = (gates - high).astype(BF16).astype(F32)
    table[8 : 8 + TOP] = high
    table[16 : 16 + TOP] = middle
    table[24 : 24 + TOP] = (gates - high) - middle
    named = table[0:8].astype(jnp.int32)
    numbers = lax.broadcasted_iota(jnp.int32, (EXPERTS, TOK), 0) + 1
    chosen_by = [numbers == named[k : k + 1] for k in range(TOP)]
    used = jnp.where(chosen_by[0], 1.0, 0.0)
    for k in range(1, TOP):
        used += jnp.where(chosen_by[k], 1.0, 0.0)
    order = lax.broadcasted_iota(jnp.int32, (TOK, TOK), 0) < lax.broadcasted_iota(
        jnp.int32, (TOK, TOK), 1
    )
    earlier = jnp.dot(
        used.astype(BF16), jnp.where(order, 1.0, 0.0).astype(BF16), preferred_element_type=F32
    )
    for k in range(TOP):
        table[32 + k : 33 + k] = jnp.sum(
            jnp.where(chosen_by[k], earlier, 0.0), axis=0, keepdims=True
        )
    tok[0, 0:TOK, width - META : width] = table[...].T.astype(BF16)
    sl[...] = jnp.zeros(sl.shape, F32)
    pl.semaphore_wait(barrier, 14)

    sends = []

    def remote(src, dst, send, recv, peer):
        return pltpu.make_async_remote_copy(
            src_ref=src,
            dst_ref=dst,
            send_sem=send,
            recv_sem=recv,
            device_id=peer,
            device_id_type=MESH,
        )

    def start(*args):
        copy = remote(*args)
        copy.start()
        sends.append(copy)

    def extra_at(slot):
        return tok.at[0, 0:TOK, pl.ds(pl.multiple_of(feats + slot * EXTRA, 128), EXTRA)]

    from_bwd, from_fwd = (3 - d) % 4, (3 + d) % 4
    mine = tok_ref.at[:, main:feats]
    start(mine, extra_at(from_bwd), e_send.at[0], e_recv.at[0], y_fwd)
    start(mine, extra_at(from_fwd), e_send.at[1], e_recv.at[1], y_bwd)
    remote(mine, extra_at(from_bwd), e_send.at[0], e_recv.at[0], y_bwd).wait_recv()
    start(extra_at(from_bwd), extra_at(1), e_send.at[2], e_recv.at[2], y_fwd)
    remote(mine, extra_at(from_fwd), e_send.at[1], e_recv.at[1], y_fwd).wait_recv()
    remote(mine, extra_at(1), e_send.at[2], e_recv.at[2], y_bwd).wait_recv()

    def own(j):
        return tok.at[j, 0:TOK]

    def other(j):
        return tok.at[j, TOK : 2 * TOK]

    def z_copy(src, dst, peer):
        return (own(src), own(dst), z_send.at[dst], z_recv.at[dst], peer)

    def row_ids(j, half, core):
        table = tok[j, half * TOK : (half + 1) * TOK, width - META : width].astype(F32).T
        expert = table[0:8].astype(jnp.int32) - 1
        slot = table[32:40].astype(jnp.int32)
        hit = (lax.shift_right_arithmetic(expert, 3) == z) & ((expert & 1) == c)
        relative = ((lax.shift_right_arithmetic(expert, 1) & 3) - x) * d & 3
        return jnp.where(hit, relative * SLAB + core * CAP + slot, -1)

    def one_hot(ids):
        rows = lax.broadcasted_iota(jnp.int32, (ROWS, TOK), 0)
        found = rows == ids[0:1]
        for k in range(1, TOP):
            found = found | (rows == ids[k : k + 1])
        return jnp.where(found, 1.0, 0.0).astype(BF16)

    def x_slab(j, xx):
        return ro.at[pl.ds(pl.multiple_of(j * ROWS + xx * SLAB, 16), SLAB)]

    def take_tokens(j):
        if j == 0:
            start(*z_copy(0, 1, z_fwd))
            start(*z_copy(0, 2, z_bwd))
        else:
            remote(*z_copy(j, j, z_fwd)).wait_recv()
            if j in (1, 3, 5):
                start(*z_copy(j, j + 2, z_fwd))
            elif j in (2, 4):
                start(*z_copy(j, j + 2, z_bwd))
        to = PARTNER_SLOT[j]
        start(own(j), other(to), c_send.at[to], c_recv.at[to], partner)

    def pack(j):
        remote(own(j), other(j), c_send.at[j], c_recv.at[j], partner).wait_recv()
        picker = jnp.concatenate([one_hot(row_ids(j, 0, c)), one_hot(row_ids(j, 1, 1 - c))], axis=1)
        here = pl.ds(pl.multiple_of(j * ROWS + x * SLAB, 16), SLAB)
        for at, size in chunks(width, 512):
            rows = jnp.dot(picker, tok[j, :, at : at + size], preferred_element_type=F32).astype(BF16)
            ro[here, at : at + size] = rows[0:SLAB]
            pk[j, :, at : at + size] = rows[SLAB:ROWS]
        for i, peer in enumerate((x_fwd, x_far, x_bwd)):
            slab = pk.at[j, i * SLAB : (i + 1) * SLAB]
            start(slab, x_slab(j, x), x_send.at[j, i], x_recv.at[j, i], peer)

    def y_block(i, j):
        return ry.at[i, j * ROWS : (j + 1) * ROWS]

    def send_y(j):
        for i, away in enumerate((-d, 2, d)):
            slab = x_slab(j, (x + away + 4) % 4)
            remote(slab, slab, x_send.at[j, i], x_recv.at[j, i], x_bwd).wait_recv()
        block = ro.at[j * ROWS : (j + 1) * ROWS, 0:main]
        start(block, y_block(0, j), y_send.at[j, 0], y_recv.at[j, 0], y_fwd)
        start(block, y_block(1, j), y_send.at[j, 1], y_recv.at[j, 1], y_bwd)

    def y_relay(j):
        remote(y_block(0, j), y_block(0, j), y_send.at[j, 0], y_recv.at[j, 0], y_bwd).wait_recv()
        start(y_block(0, j), y_block(2, j), y_send.at[j, 2], y_recv.at[j, 2], y_fwd)

    def columns(at, size):
        return pl.ds(pl.multiple_of(at, 128), size)

    owners = ((y - d + 4) % 4, (y + d + 4) % 4, (y + 2) % 4)

    def compute(j):
        for i in (1, 2):
            remote(y_block(i, j), y_block(i, j), y_send.at[j, i], y_recv.at[j, i], y_bwd).wait_recv()
        if j == 0:
            for load in loads:
                load.wait()
        rows = slice(j * ROWS, (j + 1) * ROWS)

        def times(left, at, size):
            return lax.dot_general(
                left, w[:, columns(at, size)], (((1,), (1,)), ((), ())), preferred_element_type=F32
            )

        grad = times(ro[rows, 0:feats], y * feats, feats)
        for s in range(3):
            at = feats + s * EXTRA
            owner = (y + 1 + s) % 4
            grad += times(ro[rows, at : at + EXTRA], owner * feats + main, EXTRA)
        for i in range(3):
            grad += times(ry[i, rows, :], owners[i] * feats, main)

        meta = ro[rows, width - META : width].astype(F32)
        lanes = lax.broadcasted_iota(jnp.int32, (ROWS, META), 1)
        weight = (
            pltpu.roll(meta, META - 8, 1) + pltpu.roll(meta, META - 16, 1)
        ) + pltpu.roll(meta, META - 24, 1)
        chosen = (lanes < TOP) & (meta.astype(jnp.int32) == ep + 1)
        prob = jnp.sum(jnp.where(chosen, weight, 0.0), axis=1, keepdims=True)

        zz = (z + OFFSETS[j] * d + 8) % 8
        place = pl.ds(pl.multiple_of(zz * ROWS, 16), ROWS)
        gate = sg[place, :].astype(F32)
        up = su[place, :].astype(F32)
        sigmoid = jax.nn.sigmoid(gate)
        activation = gate * sigmoid
        product = activation * up
        rounded = product.astype(BF16).astype(F32)
        hs[rows, :] = (prob * product).astype(BF16)
        part = rounded * grad
        part = part[:, 0:128] + part[:, 128:256] + part[:, 256:384]
        sl[y, pl.ds(zz, 1), 0:ROWS] = jnp.sum(part.T, axis=0, keepdims=True)
        scaled = prob * grad
        slope = sigmoid * (1.0 + gate * (1.0 - sigmoid))
        gg_ref[place, :] = (scaled * up * slope).astype(BF16)
        gu_ref[place, :] = (scaled * activation).astype(BF16)

    stage = {"T": take_tokens, "P": pack, "Y": send_y, "R": y_relay, "C": compute}
    for name in ORDER.split():
        stage[name[0]](int(name[1]))

    def wait(ref, sem):
        remote(ref, ref, s_send.at[0], sem, y_bwd).wait_recv()

    for i, peer in enumerate((y_fwd, y_far, y_bwd)):
        start(sl.at[y], sl.at[y], s_send.at[i], s_recv.at[i], peer)

    hst[...] = hs[...].T

    def weights(block, at, size):
        for piece, wide in chunks(size, 256):
            total = jnp.dot(hst[...], block(piece, wide), preferred_element_type=F32)
            gw_ref[:, columns(at + piece, wide)] = total.astype(BF16)

    weights(lambda at, size: ro[:, at : at + size], y * feats, feats)

    for i, away in enumerate((-d, 2, d)):
        wait(sl.at[(y + away + 4) % 4], s_recv.at[i])
    sums[x] = ((sl[0] + sl[1]) + sl[2]) + sl[3]
    for i, peer in enumerate((x_fwd, x_far, x_bwd)):
        start(sums.at[x], sums.at[x], s_send.at[3 + i], s_recv.at[3 + i], peer)

    for s in range(3):
        owner = (y + 1 + s) % 4
        base = feats + s * EXTRA
        weights(lambda at, size: ro[:, base + at : base + at + size], owner * feats + main, EXTRA)

    for i, away in enumerate((-d, 2, d)):
        wait(sums.at[(x + away + 4) % 4], s_recv.at[3 + i])
    start(sums, theirs, s_send.at[6], s_recv.at[6], partner)

    weights(lambda at, size: ry[0, :, at : at + size], owners[0] * feats, main)

    wait(theirs, s_recv.at[6])
    shift = (256 - (x * SLAB + c * CAP)) % 256
    for i in range(NX):
        for core in range(2):
            block = jnp.where(c == core, sums[i], theirs[i])
            zs[:, 2 * i + core, :] = pltpu.roll(block, shift, 1)[:, 0:128]
    for o in range(1, NZ):
        start(
            zs.at[(z + o) % 8],
            zr.at[z],
            b_send.at[o],
            b_recv.at[o],
            ep_at((z + o) % 8, x, c),
        )
    zr[z] = zs[z]

    for i in range(1, 3):
        weights(lambda at, size: ry[i, :, at : at + size], owners[i] * feats, main)

    for o in range(1, NZ):
        wait(zr.at[(z - o + 8) % 8], b_recv.at[o])
    back = zr[...].reshape(EXPERTS, 128)
    high = back.astype(BF16)
    rest = back - high.astype(F32)
    middle = rest.astype(BF16)
    low = (rest - middle.astype(F32)).astype(BF16)
    numbers = lax.broadcasted_iota(jnp.int32, (EXPERTS, TOK), 0) + 1
    slots = lax.broadcasted_iota(jnp.int32, (128, TOK), 0)
    named = table[0:8].astype(jnp.int32)
    wanted = table[32:40].astype(jnp.int32)
    for k in range(TOP):
        picker = jnp.where(numbers == named[k : k + 1], 1.0, 0.0).astype(BF16)
        total = jnp.zeros((128, TOK), F32)
        for part in (high, middle, low):
            total += lax.dot_general(
                part, picker, (((0,), (0,)), ((), ())), preferred_element_type=F32
            )
        back_ref[k : k + 1, :] = jnp.sum(
            jnp.where(slots == wanted[k : k + 1], total, 0.0), axis=0, keepdims=True
        )
    for copy in sends:
        copy.wait_send()


def body(grad_out, routes, gates, saved_gate, saved_up, w_down):
    experts = lax.axis_size("ep")
    feats = grad_out.shape[1]
    hidden_units = saved_gate.shape[3]
    slots = experts * CAP
    width = feats + 3 * EXTRA + META

    vmem = pl.BlockSpec(memory_space=pltpu.VMEM)
    hbm = pl.BlockSpec(memory_space=pl.ANY)
    dma = pltpu.SemaphoreType.DMA
    main = feats - EXTRA
    flops = 4 * slots * hidden_units * feats * NY
    grad_gate, grad_up, grad_w, back = pl.pallas_call(
        functools.partial(kernel, feats, width),
        out_shape=(
            jax.ShapeDtypeStruct((slots, hidden_units), BF16),
            jax.ShapeDtypeStruct((slots, hidden_units), BF16),
            jax.ShapeDtypeStruct((hidden_units, feats * NY), BF16),
            jax.ShapeDtypeStruct((TOP, TOK), F32),
        ),
        in_specs=[vmem, vmem, vmem, hbm, hbm, hbm],
        out_specs=(vmem, vmem, vmem, vmem),
        scratch_shapes=[
            pltpu.VMEM((NZ, 2 * TOK, width), BF16),
            pltpu.VMEM((NZ, 3 * SLAB, width), BF16),
            pltpu.VMEM((slots, width), BF16),
            pltpu.VMEM((3, slots, main), BF16),
            pltpu.VMEM((hidden_units, feats * NY), BF16),
            pltpu.VMEM((slots, hidden_units), BF16),
            pltpu.VMEM((slots, hidden_units), BF16),
            pltpu.VMEM((slots, hidden_units), BF16),
            pltpu.VMEM((hidden_units, slots), BF16),
            pltpu.VMEM((META, TOK), F32),
            pltpu.VMEM((NY, NZ, 256), F32),
            pltpu.VMEM((NX, NZ, 256), F32),
            pltpu.VMEM((NX, NZ, 256), F32),
            pltpu.VMEM((NZ, 8, 128), F32),
            pltpu.VMEM((NZ, 8, 128), F32),
            dma((3,)),
            dma((3,)),
            dma((3,)),
            dma((NZ,)),
            dma((NZ,)),
            dma((NZ,)),
            dma((NZ,)),
            dma((NZ, 3)),
            dma((NZ, 3)),
            dma((NZ, 3)),
            dma((NZ, 3)),
            dma((7,)),
            dma((7,)),
            dma((NZ,)),
            dma((NZ,)),
        ],
        compiler_params=pltpu.CompilerParams(
            collective_id=0, has_side_effects=True, vmem_limit_bytes=60 * 1024 * 1024
        ),
        cost_estimate=pl.CostEstimate(
            flops=flops, bytes_accessed=16 * 1024 * 1024, transcendentals=slots * hidden_units
        ),
    )(
        grad_out,
        routes.T,
        gates.T,
        saved_gate.reshape(slots, hidden_units),
        saved_up.reshape(slots, hidden_units),
        w_down[0],
    )

    return (
        grad_gate.reshape(saved_gate.shape),
        grad_up.reshape(saved_up.shape),
        grad_w[None],
        back.T,
    )


def solution(mesh):
    in_specs = (
        P("ep", "tp"),
        P("ep", None),
        P("ep", None),
        P("ep", None, None, "tp"),
        P("ep", None, None, "tp"),
        P("ep", "tp", None),
    )
    out_specs = (
        P("ep", None, None, "tp"),
        P("ep", None, None, "tp"),
        P("ep", "tp", None),
        P("ep", None),
    )
    return jax.shard_map(body, mesh=mesh, in_specs=in_specs, out_specs=out_specs, check_vma=False)
```

```python
import functools

import jax
import jax.numpy as jnp
from jax import lax
from jax.experimental import pallas as pl
from jax.experimental.pallas import tpu as pltpu
from jax.sharding import PartitionSpec as P

NZ, NX, NY = 8, 4, 4
CAP = 24
EXPERTS = 64
TOK = 128
TOP = 6
EXTRA = 384
META = 128
SLAB = 2 * CAP
PARTS = 4
ROWS = NX * SLAB
PARTNER_SLOT = (0, 2, 1, 4, 3, 6, 5, 7)
ORDER = (
    "P0 Y0 T1 T2 P1 P2 Y1 R0 T3 T4 P3 Y2 R1 C0 P4 Y3 R2 C1 T5 T6 P5 Y4 R3 C2 "
    "P6 Y5 R4 C3 T7 P7 Y6 R5 C4 Y7 R6 C5 R7 C6 C7"
)
OFFSETS = (0, -1, 1, -2, 2, -3, 3, -4)
F32 = jnp.float32
BF16 = jnp.bfloat16
MESH = pl.DeviceIdType.MESH


def chunks(total, size):
    return [(at, min(size, total - at)) for at in range(0, total, size)]


def kernel(
    feats,
    width,
    tok_ref,
    routes_ref,
    gates_ref,
    gate_hbm,
    up_hbm,
    w_hbm,
    gg_hbm,
    gu_hbm,
    gw_hbm,
    back_ref,
    tok,
    pk,
    ro,
    ry,
    w,
    sg,
    su,
    hs,
    hst,
    gg,
    gu,
    gw,
    table,
    sl,
    sums,
    theirs,
    zs,
    zr,
    in_sem,
    o_sem,
    w_sem,
    e_send,
    e_recv,
    z_send,
    z_recv,
    c_send,
    c_recv,
    x_send,
    x_recv,
    y_send,
    y_recv,
    s_send,
    s_recv,
    b_send,
    b_recv,
):
    y = lax.axis_index("tp")
    ep = lax.axis_index("ep")
    z = ep // 8
    x = (ep // 2) % 4
    c = ep % 2
    d = 1 - 2 * c
    main = feats - EXTRA
    extras = feats + META

    def ep_at(zz, xx, cc):
        return {"ep": zz * 8 + xx * 2 + cc}

    z_fwd, z_bwd = ep_at((z + d + 8) % 8, x, c), ep_at((z - d + 8) % 8, x, c)
    x_fwd, x_bwd = ep_at(z, (x + d + 4) % 4, c), ep_at(z, (x - d + 4) % 4, c)
    x_far = ep_at(z, (x + 2) % 4, c)
    y_far = {"tp": (y + 2) % 4}
    y_fwd, y_bwd = {"tp": (y + d + 4) % 4}, {"tp": (y - d + 4) % 4}
    partner = ep_at(z, x, 1 - c)

    barrier = pltpu.get_barrier_semaphore()
    z_far = [ep_at((z + o) % 8, x, c) for o in range(2, 7)]
    for peer in [z_fwd, z_bwd, x_fwd, x_far, x_bwd, y_fwd, y_far, y_bwd, partner] + z_far:
        pl.semaphore_signal(barrier, inc=1, device_id=peer, device_id_type=MESH)

    loads = [
        pltpu.make_async_copy(w_hbm, w, in_sem.at[0]),
        pltpu.make_async_copy(gate_hbm, sg, in_sem.at[1]),
        pltpu.make_async_copy(up_hbm, su, in_sem.at[2]),
    ]
    for load in loads:
        load.start()
    tok[0, 0:TOK, 0:feats] = tok_ref[...]
    table[...] = jnp.zeros((META, TOK), F32)
    table[0:TOP] = routes_ref[...].astype(F32) + 1.0
    gates = gates_ref[...]
    high = gates.astype(BF16).astype(F32)
    middle = (gates - high).astype(BF16).astype(F32)
    table[8 : 8 + TOP] = high
    table[16 : 16 + TOP] = middle
    table[24 : 24 + TOP] = (gates - high) - middle
    named = table[0:8].astype(jnp.int32)
    numbers = lax.broadcasted_iota(jnp.int32, (EXPERTS, TOK), 0) + 1
    chosen_by = [numbers == named[k : k + 1] for k in range(TOP)]
    used = jnp.where(chosen_by[0], 1.0, 0.0)
    for k in range(1, TOP):
        used += jnp.where(chosen_by[k], 1.0, 0.0)
    order = lax.broadcasted_iota(jnp.int32, (TOK, TOK), 0) < lax.broadcasted_iota(
        jnp.int32, (TOK, TOK), 1
    )
    earlier = jnp.dot(
        used.astype(BF16), jnp.where(order, 1.0, 0.0).astype(BF16), preferred_element_type=F32
    )
    for k in range(TOP):
        table[32 + k : 33 + k] = jnp.sum(
            jnp.where(chosen_by[k], earlier, 0.0), axis=0, keepdims=True
        )
    tok[0, 0:TOK, feats : feats + META] = table[...].T.astype(BF16)
    sl[...] = jnp.zeros(sl.shape, F32)
    pl.semaphore_wait(barrier, 14)

    sends = []

    def remote(src, dst, send, recv, peer):
        return pltpu.make_async_remote_copy(
            src_ref=src,
            dst_ref=dst,
            send_sem=send,
            recv_sem=recv,
            device_id=peer,
            device_id_type=MESH,
        )

    def start(*args):
        copy = remote(*args)
        copy.start()
        sends.append(copy)

    def extra_at(slot):
        return tok.at[0, 0:TOK, pl.ds(pl.multiple_of(extras + slot * EXTRA, 128), EXTRA)]

    here = tok.at[0, 0:TOK, 0:extras]
    for j, peer in ((1, z_fwd), (2, z_bwd)):
        start(here, tok.at[j, 0:TOK, 0:extras], z_send.at[j], z_recv.at[j], peer)
    mine = tok_ref.at[:, main:feats]
    slots = ((3 - d) % 4, 1, (3 + d) % 4)
    for i, peer in enumerate((y_fwd, y_far, y_bwd)):
        start(mine, extra_at(slots[i]), e_send.at[i], e_recv.at[i], peer)

    def own(j):
        return tok.at[j, 0:TOK]

    def other(j):
        return tok.at[j, TOK : 2 * TOK]

    def z_copy(src, dst, peer):
        return (own(src), own(dst), z_send.at[dst], z_recv.at[dst], peer)

    def row_ids(j, half, core):
        table = tok[j, half * TOK : (half + 1) * TOK, feats : feats + META].astype(F32).T
        expert = table[0:8].astype(jnp.int32) - 1
        slot = table[32:40].astype(jnp.int32)
        hit = (lax.shift_right_arithmetic(expert, 3) == z) & ((expert & 1) == c)
        relative = ((lax.shift_right_arithmetic(expert, 1) & 3) - x) * d & 3
        return jnp.where(hit, relative * SLAB + core * CAP + slot, -1)

    def one_hot(ids):
        rows = lax.broadcasted_iota(jnp.int32, (ROWS, TOK), 0)
        found = rows == ids[0:1]
        for k in range(1, TOP):
            found = found | (rows == ids[k : k + 1])
        return jnp.where(found, 1.0, 0.0).astype(BF16)

    def x_slab(j, xx):
        return ro.at[pl.ds(pl.multiple_of(j * ROWS + xx * SLAB, 16), SLAB)]

    def exchange(part, sem):
        return (
            tok.at[0, 0:TOK, part],
            tok.at[0, TOK : 2 * TOK, part],
            c_send.at[sem],
            c_recv.at[sem],
            partner,
        )

    def take_tokens(j):
        if j in (1, 2):
            for part, sem in ((slice(0, extras), z_recv.at[j]), (slice(extras, width), e_recv.at[2 + j])):
                ref = tok.at[j, 0:TOK, part]
                remote(ref, ref, z_send.at[j], sem, z_fwd).wait_recv()
        else:
            remote(*z_copy(j, j, z_fwd)).wait_recv()
        if j in (1, 3, 5):
            start(*z_copy(j, j + 2, z_fwd))
        elif j in (2, 4):
            start(*z_copy(j, j + 2, z_bwd))
        to = PARTNER_SLOT[j]
        start(own(j), other(to), c_send.at[to], c_recv.at[to], partner)

    pieces = (slice(0, main), slice(main, width))

    def pack(j):
        if j > 0:
            remote(own(j), other(j), c_send.at[j], c_recv.at[j], partner).wait_recv()
        else:
            start(*exchange(slice(0, extras), 0))
            remote(*exchange(slice(0, extras), 0)).wait_recv()
        picker = jnp.concatenate([one_hot(row_ids(j, 0, c)), one_hot(row_ids(j, 1, 1 - c))], axis=1)
        here = pl.ds(pl.multiple_of(j * ROWS + x * SLAB, 16), SLAB)
        for p, piece in enumerate(pieces):
            if j == 0 and p == 1:
                for i in range(3):
                    remote(mine, extra_at(slots[i]), e_send.at[i], e_recv.at[i], y_bwd).wait_recv()
                gathered = tok.at[0, 0:TOK, extras:width]
                for k, peer in ((1, z_fwd), (2, z_bwd)):
                    part = tok.at[k, 0:TOK, extras:width]
                    start(gathered, part, e_send.at[2 + k], e_recv.at[2 + k], peer)
                start(*exchange(slice(extras, width), NZ))
                remote(*exchange(slice(extras, width), NZ)).wait_recv()
            for at, size in chunks(piece.stop - piece.start, 512):
                columns = slice(piece.start + at, piece.start + at + size)
                rows = jnp.dot(picker, tok[j, :, columns], preferred_element_type=F32).astype(BF16)
                ro[here, columns] = rows[0:SLAB]
                pk[j, :, columns] = rows[SLAB:ROWS]
            for i, peer in enumerate((x_fwd, x_far, x_bwd)):
                slab = pk.at[j, i * SLAB : (i + 1) * SLAB, piece]
                sem = 3 * p + i
                start(slab, x_slab(j, x).at[:, piece], x_send.at[j, sem], x_recv.at[j, sem], peer)

    def wait_x(j, p):
        for i, away in enumerate((-d, 2, d)):
            slab = x_slab(j, (x + away + 4) % 4).at[:, pieces[p]]
            remote(slab, slab, x_send.at[j, i], x_recv.at[j, 3 * p + i], x_bwd).wait_recv()

    def y_block(i, j):
        return ry.at[i, j * ROWS : (j + 1) * ROWS]

    def send_y(j):
        wait_x(j, 0)
        block = ro.at[j * ROWS : (j + 1) * ROWS, 0:main]
        start(block, y_block(0, j), y_send.at[j, 0], y_recv.at[j, 0], y_fwd)
        start(block, y_block(1, j), y_send.at[j, 1], y_recv.at[j, 1], y_bwd)

    def y_relay(j):
        remote(y_block(0, j), y_block(0, j), y_send.at[j, 0], y_recv.at[j, 0], y_bwd).wait_recv()
        start(y_block(0, j), y_block(2, j), y_send.at[j, 2], y_recv.at[j, 2], y_fwd)

    stores = []

    def store(src, dst, sem):
        copy = pltpu.make_async_copy(src, dst, sem)
        copy.start()
        stores.append(copy)

    def columns(at, size):
        return pl.ds(pl.multiple_of(at, 128), size)

    owners = ((y - d + 4) % 4, (y + d + 4) % 4, (y + 2) % 4)

    def compute(j):
        if j == 0:
            for load in loads:
                load.wait()
        wait_x(j, 1)
        rows = slice(j * ROWS, (j + 1) * ROWS)

        def times(left, at, size):
            return lax.dot_general(
                left, w[:, columns(at, size)], (((1,), (1,)), ((), ())), preferred_element_type=F32
            )

        grad = times(ro[rows, 0:feats], y * feats, feats)
        for s in range(3):
            at = extras + s * EXTRA
            owner = (y + 1 + s) % 4
            grad += times(ro[rows, at : at + EXTRA], owner * feats + main, EXTRA)
        for i in range(3):
            if i > 0:
                block = y_block(i, j)
                remote(block, block, y_send.at[j, i], y_recv.at[j, i], y_bwd).wait_recv()
            grad += times(ry[i, rows, :], owners[i] * feats, main)

        meta = ro[rows, feats : feats + META].astype(F32)
        lanes = lax.broadcasted_iota(jnp.int32, (ROWS, META), 1)
        weight = (
            pltpu.roll(meta, META - 8, 1) + pltpu.roll(meta, META - 16, 1)
        ) + pltpu.roll(meta, META - 24, 1)
        chosen = (lanes < TOP) & (meta.astype(jnp.int32) == ep + 1)
        prob = jnp.sum(jnp.where(chosen, weight, 0.0), axis=1, keepdims=True)

        zz = (z + OFFSETS[j] * d + 8) % 8
        place = pl.ds(pl.multiple_of(zz * ROWS, 16), ROWS)
        gate = sg[place, :].astype(F32)
        up = su[place, :].astype(F32)
        sigmoid = jax.nn.sigmoid(gate)
        activation = gate * sigmoid
        product = activation * up
        rounded = product.astype(BF16).astype(F32)
        hs[rows, :] = (prob * product).astype(BF16)
        part = rounded * grad
        part = part[:, 0:128] + part[:, 128:256] + part[:, 256:384]
        sl[y, pl.ds(zz, 1), 0:ROWS] = jnp.sum(part.T, axis=0, keepdims=True)
        scaled = prob * grad
        slope = sigmoid * (1.0 + gate * (1.0 - sigmoid))
        gg[place, :] = (scaled * up * slope).astype(BF16)
        gu[place, :] = (scaled * activation).astype(BF16)
        store(gg.at[place], gg_hbm.at[place], o_sem.at[j, 0])
        store(gu.at[place], gu_hbm.at[place], o_sem.at[j, 1])

    stage = {"T": take_tokens, "P": pack, "Y": send_y, "R": y_relay, "C": compute}
    for name in ORDER.split():
        stage[name[0]](int(name[1]))

    def wait(ref, sem):
        remote(ref, ref, s_send.at[0], sem, y_bwd).wait_recv()

    for i, peer in enumerate((y_fwd, y_far, y_bwd)):
        start(sl.at[y], sl.at[y], s_send.at[i], s_recv.at[i], peer)

    hst[...] = hs[...].T

    def weights(block, at, size):
        for piece, wide in chunks(size, 256):
            total = jnp.dot(hst[...], block(piece, wide), preferred_element_type=F32)
            gw[:, columns(at + piece, wide)] = total.astype(BF16)
        done = columns(at, size)
        store(gw.at[:, done], gw_hbm.at[:, done], w_sem.at[len(stores) - 2 * NZ])

    weights(lambda at, size: ro[:, at : at + size], y * feats, feats)

    for i, away in enumerate((-d, 2, d)):
        wait(sl.at[(y + away + 4) % 4], s_recv.at[i])
    sums[x] = ((sl[0] + sl[1]) + sl[2]) + sl[3]
    for i, peer in enumerate((x_fwd, x_far, x_bwd)):
        start(sums.at[x], sums.at[x], s_send.at[3 + i], s_recv.at[3 + i], peer)

    for s in range(3):
        owner = (y + 1 + s) % 4
        base = extras + s * EXTRA
        weights(lambda at, size: ro[:, base + at : base + at + size], owner * feats + main, EXTRA)

    for i, away in enumerate((-d, 2, d)):
        wait(sums.at[(x + away + 4) % 4], s_recv.at[3 + i])
    start(sums, theirs, s_send.at[6], s_recv.at[6], partner)

    weights(lambda at, size: ry[0, :, at : at + size], owners[0] * feats, main)

    wait(theirs, s_recv.at[6])
    shift = (256 - (x * SLAB + c * CAP)) % 256
    for i in range(NX):
        for core in range(2):
            block = jnp.where(c == core, sums[i], theirs[i])
            zs[:, 2 * i + core, :] = pltpu.roll(block, shift, 1)[:, 0:128]
    for o in range(1, NZ):
        start(
            zs.at[(z + o) % 8],
            zr.at[z],
            b_send.at[o],
            b_recv.at[o],
            ep_at((z + o) % 8, x, c),
        )
    zr[z] = zs[z]

    for i in range(1, 3):
        weights(lambda at, size: ry[i, :, at : at + size], owners[i] * feats, main)

    for o in range(1, NZ):
        wait(zr.at[(z - o + 8) % 8], b_recv.at[o])
    back = zr[...].reshape(EXPERTS, 128)
    high = back.astype(BF16)
    rest = back - high.astype(F32)
    middle = rest.astype(BF16)
    low = (rest - middle.astype(F32)).astype(BF16)
    numbers = lax.broadcasted_iota(jnp.int32, (EXPERTS, TOK), 0) + 1
    slots = lax.broadcasted_iota(jnp.int32, (128, TOK), 0)
    named = table[0:8].astype(jnp.int32)
    wanted = table[32:40].astype(jnp.int32)
    for k in range(TOP):
        picker = jnp.where(numbers == named[k : k + 1], 1.0, 0.0).astype(BF16)
        total = jnp.zeros((128, TOK), F32)
        for part in (high, middle, low):
            total += lax.dot_general(
                part, picker, (((0,), (0,)), ((), ())), preferred_element_type=F32
            )
        back_ref[k : k + 1, :] = jnp.sum(
            jnp.where(slots == wanted[k : k + 1], total, 0.0), axis=0, keepdims=True
        )
    for copy in stores:
        copy.wait()
    for copy in sends:
        copy.wait_send()


def hand_over(*refs):
    arrays = 3
    inputs, small_in, outputs, small_out = refs[0:3], refs[3], refs[4:7], refs[7]
    held, sem = refs[8:11], refs[11]
    loads, stores = [], []
    for i in range(arrays):
        size = inputs[i].shape[0] // PARTS
        for part in range(PARTS):
            rows = pl.ds(part * size, size)
            loads.append(
                pltpu.make_async_copy(inputs[i].at[rows], held[i].at[rows], sem.at[0, i, part])
            )
            stores.append(
                pltpu.make_async_copy(held[i].at[rows], outputs[i].at[rows], sem.at[1, i, part])
            )
    for load in loads:
        load.start()
    small_out[...] = small_in[...]
    for load, store in zip(loads, stores):
        load.wait()
        store.start()
    for store in stores:
        store.wait()


def body(grad_out, routes, gates, saved_gate, saved_up, w_down):
    experts = lax.axis_size("ep")
    feats = grad_out.shape[1]
    hidden_units = saved_gate.shape[3]
    slots = experts * CAP
    width = feats + 3 * EXTRA + META

    vmem = pl.BlockSpec(memory_space=pltpu.VMEM)
    hbm = pl.BlockSpec(memory_space=pl.ANY)
    dma = pltpu.SemaphoreType.DMA
    main = feats - EXTRA
    flops = 4 * slots * hidden_units * feats * NY
    grad_gate, grad_up, grad_w, back = pl.pallas_call(
        functools.partial(kernel, feats, width),
        out_shape=(
            jax.ShapeDtypeStruct((slots, hidden_units), BF16),
            jax.ShapeDtypeStruct((slots, hidden_units), BF16),
            jax.ShapeDtypeStruct((hidden_units, feats * NY), BF16),
            jax.ShapeDtypeStruct((TOP, TOK), F32),
        ),
        in_specs=[vmem, vmem, vmem, hbm, hbm, hbm],
        out_specs=(hbm, hbm, hbm, vmem),
        scratch_shapes=[
            pltpu.VMEM((NZ, 2 * TOK, width), BF16),
            pltpu.VMEM((NZ, 3 * SLAB, width), BF16),
            pltpu.VMEM((slots, width), BF16),
            pltpu.VMEM((3, slots, main), BF16),
            pltpu.VMEM((hidden_units, feats * NY), BF16),
            pltpu.VMEM((slots, hidden_units), BF16),
            pltpu.VMEM((slots, hidden_units), BF16),
            pltpu.VMEM((slots, hidden_units), BF16),
            pltpu.VMEM((hidden_units, slots), BF16),
            pltpu.VMEM((slots, hidden_units), BF16),
            pltpu.VMEM((slots, hidden_units), BF16),
            pltpu.VMEM((hidden_units, feats * NY), BF16),
            pltpu.VMEM((META, TOK), F32),
            pltpu.VMEM((NY, NZ, 256), F32),
            pltpu.VMEM((NX, NZ, 256), F32),
            pltpu.VMEM((NX, NZ, 256), F32),
            pltpu.VMEM((NZ, 8, 128), F32),
            pltpu.VMEM((NZ, 8, 128), F32),
            dma((3,)),
            dma((NZ, 2)),
            dma((7,)),
            dma((5,)),
            dma((5,)),
            dma((NZ,)),
            dma((NZ,)),
            dma((NZ + 1,)),
            dma((NZ + 1,)),
            dma((NZ, 6)),
            dma((NZ, 6)),
            dma((NZ, 3)),
            dma((NZ, 3)),
            dma((7,)),
            dma((7,)),
            dma((NZ,)),
            dma((NZ,)),
        ],
        compiler_params=pltpu.CompilerParams(
            collective_id=0, has_side_effects=True, vmem_limit_bytes=60 * 1024 * 1024
        ),
        cost_estimate=pl.CostEstimate(
            flops=flops, bytes_accessed=16 * 1024 * 1024, transcendentals=slots * hidden_units
        ),
    )(
        grad_out,
        routes.T,
        gates.T,
        saved_gate.reshape(slots, hidden_units),
        saved_up.reshape(slots, hidden_units),
        w_down[0],
    )

    results = (grad_gate, grad_up, grad_w, back)
    grad_gate, grad_up, grad_w, back = pl.pallas_call(
        hand_over,
        out_shape=tuple(jax.ShapeDtypeStruct(a.shape, a.dtype) for a in results),
        in_specs=[hbm, hbm, hbm, vmem],
        out_specs=(hbm, hbm, hbm, vmem),
        scratch_shapes=[pltpu.VMEM(a.shape, a.dtype) for a in results[0:3]] + [dma((2, 3, PARTS))],
    )(*results)
    return (
        grad_gate.reshape(saved_gate.shape),
        grad_up.reshape(saved_up.shape),
        grad_w[None],
        back.T,
    )


def solution(mesh):
    in_specs = (
        P("ep", "tp"),
        P("ep", None),
        P("ep", None),
        P("ep", None, None, "tp"),
        P("ep", None, None, "tp"),
        P("ep", "tp", None),
    )
    out_specs = (
        P("ep", None, None, "tp"),
        P("ep", None, None, "tp"),
        P("ep", "tp", None),
        P("ep", None),
    )
    return jax.shard_map(body, mesh=mesh, in_specs=in_specs, out_specs=out_specs, check_vma=False)
```

```python
import functools

import jax
import jax.numpy as jnp
from jax import lax
from jax.experimental import pallas as pl
from jax.experimental.pallas import tpu as pltpu
from jax.sharding import PartitionSpec as P

NZ, NX, NY = 8, 4, 4
CAP = 24
EXPERTS = 64
TOK = 128
TOP = 6
EXTRA = 384
META = 128
SLAB = 2 * CAP
PARTS = 4
ROWS = NX * SLAB
PARTNER_SLOT = (0, 2, 1, 4, 3, 6, 5, 7)
ORDER = (
    "P0 Y0 T1 T2 P1 P2 Y1 R0 T3 T4 P3 Y2 R1 C0 P4 Y3 R2 C1 T5 T6 P5 Y4 R3 C2 "
    "P6 Y5 R4 C3 T7 P7 Y6 R5 C4 Y7 R6 C5 R7 C6 C7"
)
OFFSETS = (0, -1, 1, -2, 2, -3, 3, -4)
F32 = jnp.float32
BF16 = jnp.bfloat16
MESH = pl.DeviceIdType.MESH


def chunks(total, size):
    return [(at, min(size, total - at)) for at in range(0, total, size)]


def kernel(
    feats,
    width,
    tok_ref,
    routes_ref,
    gates_ref,
    gate_hbm,
    up_hbm,
    w_hbm,
    gg,
    gu,
    gw,
    back_ref,
    tok,
    pk,
    ro,
    ry,
    w,
    sg,
    su,
    hs,
    hst,
    table,
    sl,
    sums,
    zs,
    zr,
    in_sem,
    e_send,
    e_recv,
    z_send,
    z_recv,
    c_send,
    c_recv,
    x_send,
    x_recv,
    y_send,
    y_recv,
    s_send,
    s_recv,
    b_send,
    b_recv,
):
    y = lax.axis_index("tp")
    ep = lax.axis_index("ep")
    z = ep // 8
    x = (ep // 2) % 4
    c = ep % 2
    d = 1 - 2 * c
    main = feats - EXTRA
    extras = feats + META

    def ep_at(zz, xx, cc):
        return {"ep": zz * 8 + xx * 2 + cc}

    z_fwd, z_bwd = ep_at((z + d + 8) % 8, x, c), ep_at((z - d + 8) % 8, x, c)
    x_fwd, x_bwd = ep_at(z, (x + d + 4) % 4, c), ep_at(z, (x - d + 4) % 4, c)
    x_far = ep_at(z, (x + 2) % 4, c)
    y_far = {"tp": (y + 2) % 4}
    y_fwd, y_bwd = {"tp": (y + d + 4) % 4}, {"tp": (y - d + 4) % 4}
    partner = ep_at(z, x, 1 - c)

    barrier = pltpu.get_barrier_semaphore()
    z_far = [ep_at((z + o) % 8, x, c) for o in range(2, 7)]
    x_other = [ep_at(z, (x + o) % 4, 1 - c) for o in range(1, NX)]
    peers = [z_fwd, z_bwd, x_fwd, x_far, x_bwd, y_fwd, y_far, y_bwd, partner]
    for peer in peers + z_far + x_other:
        pl.semaphore_signal(barrier, inc=1, device_id=peer, device_id_type=MESH)

    loads = [
        pltpu.make_async_copy(w_hbm, w, in_sem.at[0]),
        pltpu.make_async_copy(gate_hbm, sg, in_sem.at[1]),
        pltpu.make_async_copy(up_hbm, su, in_sem.at[2]),
    ]
    for load in loads:
        load.start()
    tok[0, 0:TOK, 0:feats] = tok_ref[...]
    table[...] = jnp.zeros((META, TOK), F32)
    table[0:TOP] = routes_ref[...].astype(F32) + 1.0
    gates = gates_ref[...]
    high = gates.astype(BF16).astype(F32)
    middle = (gates - high).astype(BF16).astype(F32)
    table[8 : 8 + TOP] = high
    table[16 : 16 + TOP] = middle
    table[24 : 24 + TOP] = (gates - high) - middle
    named = table[0:8].astype(jnp.int32)
    numbers = lax.broadcasted_iota(jnp.int32, (EXPERTS, TOK), 0) + 1
    chosen_by = [numbers == named[k : k + 1] for k in range(TOP)]
    used = jnp.where(chosen_by[0], 1.0, 0.0)
    for k in range(1, TOP):
        used += jnp.where(chosen_by[k], 1.0, 0.0)
    order = lax.broadcasted_iota(jnp.int32, (TOK, TOK), 0) < lax.broadcasted_iota(
        jnp.int32, (TOK, TOK), 1
    )
    earlier = jnp.dot(
        used.astype(BF16), jnp.where(order, 1.0, 0.0).astype(BF16), preferred_element_type=F32
    )
    for k in range(TOP):
        table[32 + k : 33 + k] = jnp.sum(
            jnp.where(chosen_by[k], earlier, 0.0), axis=0, keepdims=True
        )
    tok[0, 0:TOK, feats : feats + META] = table[...].T.astype(BF16)
    sl[...] = jnp.zeros(sl.shape, F32)
    pl.semaphore_wait(barrier, 17)

    sends = []

    def remote(src, dst, send, recv, peer):
        return pltpu.make_async_remote_copy(
            src_ref=src,
            dst_ref=dst,
            send_sem=send,
            recv_sem=recv,
            device_id=peer,
            device_id_type=MESH,
        )

    def start(*args):
        copy = remote(*args)
        copy.start()
        sends.append(copy)

    def extra_at(slot):
        return tok.at[0, 0:TOK, pl.ds(pl.multiple_of(extras + slot * EXTRA, 128), EXTRA)]

    here = tok.at[0, 0:TOK, 0:extras]
    for j, peer in ((1, z_fwd), (2, z_bwd)):
        start(here, tok.at[j, 0:TOK, 0:extras], z_send.at[j], z_recv.at[j], peer)
    mine = tok_ref.at[:, main:feats]
    slots = ((3 - d) % 4, 1, (3 + d) % 4)
    for i, peer in enumerate((y_fwd, y_far, y_bwd)):
        start(mine, extra_at(slots[i]), e_send.at[i], e_recv.at[i], peer)

    def own(j):
        return tok.at[j, 0:TOK]

    def other(j):
        return tok.at[j, TOK : 2 * TOK]

    def z_copy(src, dst, peer):
        return (own(src), own(dst), z_send.at[dst], z_recv.at[dst], peer)

    def row_ids(j, half, core):
        table = tok[j, half * TOK : (half + 1) * TOK, feats : feats + META].astype(F32).T
        expert = table[0:8].astype(jnp.int32) - 1
        slot = table[32:40].astype(jnp.int32)
        hit = (lax.shift_right_arithmetic(expert, 3) == z) & ((expert & 1) == c)
        relative = ((lax.shift_right_arithmetic(expert, 1) & 3) - x) * d & 3
        return jnp.where(hit, relative * SLAB + core * CAP + slot, -1)

    def one_hot(ids):
        rows = lax.broadcasted_iota(jnp.int32, (ROWS, TOK), 0)
        found = rows == ids[0:1]
        for k in range(1, TOP):
            found = found | (rows == ids[k : k + 1])
        return jnp.where(found, 1.0, 0.0).astype(BF16)

    def x_slab(j, xx):
        return ro.at[pl.ds(pl.multiple_of(j * ROWS + xx * SLAB, 16), SLAB)]

    def exchange(part, sem):
        return (
            tok.at[0, 0:TOK, part],
            tok.at[0, TOK : 2 * TOK, part],
            c_send.at[sem],
            c_recv.at[sem],
            partner,
        )

    def take_tokens(j):
        if j in (1, 2):
            for part, sem in ((slice(0, extras), z_recv.at[j]), (slice(extras, width), e_recv.at[2 + j])):
                ref = tok.at[j, 0:TOK, part]
                remote(ref, ref, z_send.at[j], sem, z_fwd).wait_recv()
        else:
            remote(*z_copy(j, j, z_fwd)).wait_recv()
        if j in (1, 3, 5):
            start(*z_copy(j, j + 2, z_fwd))
        elif j in (2, 4):
            start(*z_copy(j, j + 2, z_bwd))
        to = PARTNER_SLOT[j]
        start(own(j), other(to), c_send.at[to], c_recv.at[to], partner)

    pieces = (slice(0, main), slice(main, width))

    def pack(j):
        if j > 0:
            remote(own(j), other(j), c_send.at[j], c_recv.at[j], partner).wait_recv()
        else:
            start(*exchange(slice(0, extras), 0))
            remote(*exchange(slice(0, extras), 0)).wait_recv()
        picker = jnp.concatenate([one_hot(row_ids(j, 0, c)), one_hot(row_ids(j, 1, 1 - c))], axis=1)
        here = pl.ds(pl.multiple_of(j * ROWS + x * SLAB, 16), SLAB)
        for p, piece in enumerate(pieces):
            if j == 0 and p == 1:
                for i in range(3):
                    remote(mine, extra_at(slots[i]), e_send.at[i], e_recv.at[i], y_bwd).wait_recv()
                gathered = tok.at[0, 0:TOK, extras:width]
                for k, peer in ((1, z_fwd), (2, z_bwd)):
                    part = tok.at[k, 0:TOK, extras:width]
                    start(gathered, part, e_send.at[2 + k], e_recv.at[2 + k], peer)
                start(*exchange(slice(extras, width), NZ))
                remote(*exchange(slice(extras, width), NZ)).wait_recv()
            for at, size in chunks(piece.stop - piece.start, 512):
                columns = slice(piece.start + at, piece.start + at + size)
                rows = jnp.dot(picker, tok[j, :, columns], preferred_element_type=F32).astype(BF16)
                ro[here, columns] = rows[0:SLAB]
                pk[j, :, columns] = rows[SLAB:ROWS]
            for i, peer in enumerate((x_fwd, x_far, x_bwd)):
                slab = pk.at[j, i * SLAB : (i + 1) * SLAB, piece]
                sem = 3 * p + i
                start(slab, x_slab(j, x).at[:, piece], x_send.at[j, sem], x_recv.at[j, sem], peer)

    def wait_x(j, p):
        for i, away in enumerate((-d, 2, d)):
            slab = x_slab(j, (x + away + 4) % 4).at[:, pieces[p]]
            remote(slab, slab, x_send.at[j, i], x_recv.at[j, 3 * p + i], x_bwd).wait_recv()

    def y_block(i, j):
        return ry.at[i, j * ROWS : (j + 1) * ROWS]

    def send_y(j):
        wait_x(j, 0)
        block = ro.at[j * ROWS : (j + 1) * ROWS, 0:main]
        start(block, y_block(0, j), y_send.at[j, 0], y_recv.at[j, 0], y_fwd)
        start(block, y_block(1, j), y_send.at[j, 1], y_recv.at[j, 1], y_bwd)

    def y_relay(j):
        remote(y_block(0, j), y_block(0, j), y_send.at[j, 0], y_recv.at[j, 0], y_bwd).wait_recv()
        start(y_block(0, j), y_block(2, j), y_send.at[j, 2], y_recv.at[j, 2], y_fwd)

    def columns(at, size):
        return pl.ds(pl.multiple_of(at, 128), size)

    owners = ((y - d + 4) % 4, (y + d + 4) % 4, (y + 2) % 4)

    def compute(j):
        if j == 0:
            for load in loads:
                load.wait()
        wait_x(j, 1)
        rows = slice(j * ROWS, (j + 1) * ROWS)

        def times(left, at, size):
            return lax.dot_general(
                left, w[:, columns(at, size)], (((1,), (1,)), ((), ())), preferred_element_type=F32
            )

        grad = times(ro[rows, 0:feats], y * feats, feats)
        for s in range(3):
            at = extras + s * EXTRA
            owner = (y + 1 + s) % 4
            grad += times(ro[rows, at : at + EXTRA], owner * feats + main, EXTRA)
        for i in range(3):
            if i > 0:
                block = y_block(i, j)
                remote(block, block, y_send.at[j, i], y_recv.at[j, i], y_bwd).wait_recv()
            grad += times(ry[i, rows, :], owners[i] * feats, main)

        meta = ro[rows, feats : feats + META].astype(F32)
        lanes = lax.broadcasted_iota(jnp.int32, (ROWS, META), 1)
        weight = (
            pltpu.roll(meta, META - 8, 1) + pltpu.roll(meta, META - 16, 1)
        ) + pltpu.roll(meta, META - 24, 1)
        chosen = (lanes < TOP) & (meta.astype(jnp.int32) == ep + 1)
        prob = jnp.sum(jnp.where(chosen, weight, 0.0), axis=1, keepdims=True)

        zz = (z + OFFSETS[j] * d + 8) % 8
        place = pl.ds(pl.multiple_of(zz * ROWS, 16), ROWS)
        gate = sg[place, :].astype(F32)
        up = su[place, :].astype(F32)
        sigmoid = jax.nn.sigmoid(gate)
        activation = gate * sigmoid
        product = activation * up
        rounded = product.astype(BF16).astype(F32)
        hs[rows, :] = (prob * product).astype(BF16)
        part = rounded * grad
        part = part[:, 0:128] + part[:, 128:256] + part[:, 256:384]
        sl[y, pl.ds(zz, 1), 0:ROWS] = jnp.sum(part.T, axis=0, keepdims=True)
        scaled = prob * grad
        slope = sigmoid * (1.0 + gate * (1.0 - sigmoid))
        gg[place, :] = (scaled * up * slope).astype(BF16)
        gu[place, :] = (scaled * activation).astype(BF16)

    stage = {"T": take_tokens, "P": pack, "Y": send_y, "R": y_relay, "C": compute}
    for name in ORDER.split():
        stage[name[0]](int(name[1]))

    def wait(ref, sem):
        remote(ref, ref, s_send.at[0], sem, y_bwd).wait_recv()

    for i, peer in enumerate((y_fwd, y_far, y_bwd)):
        start(sl.at[y], sl.at[y], s_send.at[i], s_recv.at[i], peer)

    hst[...] = hs[...].T

    def weights(block, at, size):
        for piece, wide in chunks(size, 256):
            total = jnp.dot(hst[...], block(piece, wide), preferred_element_type=F32)
            gw[:, columns(at + piece, wide)] = total.astype(BF16)

    weights(lambda at, size: ro[:, at : at + size], y * feats, feats)

    for i, away in enumerate((-d, 2, d)):
        wait(sl.at[(y + away + 4) % 4], s_recv.at[i])
    me = 2 * x + c
    sums[me] = ((sl[0] + sl[1]) + sl[2]) + sl[3]
    for o in range(1, 2 * NX):
        peer = ep_at(z, (x + o // 2) % 4, (c + o) % 2)
        start(sums.at[me], sums.at[me], s_send.at[2 + o], s_recv.at[2 + o], peer)

    for s in range(3):
        owner = (y + 1 + s) % 4
        base = extras + s * EXTRA
        weights(lambda at, size: ro[:, base + at : base + at + size], owner * feats + main, EXTRA)

    for o in range(1, 2 * NX):
        wait(sums.at[2 * ((x - o // 2 + 4) % 4) + (c + o) % 2], s_recv.at[2 + o])
    shift = (256 - (x * SLAB + c * CAP)) % 256
    for i in range(2 * NX):
        zs[:, i, :] = pltpu.roll(sums[i], shift, 1)[:, 0:128]
    for o in range(1, NZ):
        start(
            zs.at[(z + o) % 8],
            zr.at[z],
            b_send.at[o],
            b_recv.at[o],
            ep_at((z + o) % 8, x, c),
        )
    zr[z] = zs[z]

    for i in range(3):
        weights(lambda at, size: ry[i, :, at : at + size], owners[i] * feats, main)

    for o in range(1, NZ):
        wait(zr.at[(z - o + 8) % 8], b_recv.at[o])
    back = zr[...].reshape(EXPERTS, 128)
    high = back.astype(BF16)
    rest = back - high.astype(F32)
    middle = rest.astype(BF16)
    low = (rest - middle.astype(F32)).astype(BF16)
    numbers = lax.broadcasted_iota(jnp.int32, (EXPERTS, TOK), 0) + 1
    slots = lax.broadcasted_iota(jnp.int32, (128, TOK), 0)
    named = table[0:8].astype(jnp.int32)
    wanted = table[32:40].astype(jnp.int32)
    for k in range(TOP):
        picker = jnp.where(numbers == named[k : k + 1], 1.0, 0.0).astype(BF16)
        total = jnp.zeros((128, TOK), F32)
        for part in (high, middle, low):
            total += lax.dot_general(
                part, picker, (((0,), (0,)), ((), ())), preferred_element_type=F32
            )
        back_ref[k : k + 1, :] = jnp.sum(
            jnp.where(slots == wanted[k : k + 1], total, 0.0), axis=0, keepdims=True
        )
    for copy in sends:
        copy.wait_send()


def hand_over(*refs):
    inputs, small_in, outputs, small_out, sem = refs[0:3], refs[3], refs[4:7], refs[7], refs[8]
    copies = []
    for i in range(3):
        size = inputs[i].shape[0] // PARTS
        for part in range(PARTS):
            rows = pl.ds(part * size, size)
            copies.append(
                pltpu.make_async_copy(inputs[i].at[rows], outputs[i].at[rows], sem.at[i, part])
            )
    for copy in copies:
        copy.start()
    small_out[...] = small_in[...]
    for copy in copies:
        copy.wait()


def body(grad_out, routes, gates, saved_gate, saved_up, w_down):
    experts = lax.axis_size("ep")
    feats = grad_out.shape[1]
    hidden_units = saved_gate.shape[3]
    slots = experts * CAP
    width = feats + 3 * EXTRA + META

    vmem = pl.BlockSpec(memory_space=pltpu.VMEM)
    hbm = pl.BlockSpec(memory_space=pl.ANY)
    dma = pltpu.SemaphoreType.DMA
    main = feats - EXTRA
    flops = 4 * slots * hidden_units * feats * NY
    grad_gate, grad_up, grad_w, back = pl.pallas_call(
        functools.partial(kernel, feats, width),
        out_shape=(
            pltpu.VMEM((slots, hidden_units), BF16),
            pltpu.VMEM((slots, hidden_units), BF16),
            pltpu.VMEM((hidden_units, feats * NY), BF16),
            jax.ShapeDtypeStruct((TOP, TOK), F32),
        ),
        in_specs=[vmem, vmem, vmem, hbm, hbm, hbm],
        out_specs=(vmem, vmem, vmem, vmem),
        scratch_shapes=[
            pltpu.VMEM((NZ, 2 * TOK, width), BF16),
            pltpu.VMEM((NZ, 3 * SLAB, width), BF16),
            pltpu.VMEM((slots, width), BF16),
            pltpu.VMEM((3, slots, main), BF16),
            pltpu.VMEM((hidden_units, feats * NY), BF16),
            pltpu.VMEM((slots, hidden_units), BF16),
            pltpu.VMEM((slots, hidden_units), BF16),
            pltpu.VMEM((slots, hidden_units), BF16),
            pltpu.VMEM((hidden_units, slots), BF16),
            pltpu.VMEM((META, TOK), F32),
            pltpu.VMEM((NY, NZ, 256), F32),
            pltpu.VMEM((2 * NX, NZ, 256), F32),
            pltpu.VMEM((NZ, 8, 128), F32),
            pltpu.VMEM((NZ, 8, 128), F32),
            dma((3,)),
            dma((5,)),
            dma((5,)),
            dma((NZ,)),
            dma((NZ,)),
            dma((NZ + 1,)),
            dma((NZ + 1,)),
            dma((NZ, 6)),
            dma((NZ, 6)),
            dma((NZ, 3)),
            dma((NZ, 3)),
            dma((2 + 2 * NX,)),
            dma((2 + 2 * NX,)),
            dma((NZ,)),
            dma((NZ,)),
        ],
        compiler_params=pltpu.CompilerParams(
            collective_id=0, has_side_effects=True, vmem_limit_bytes=52 * 1024 * 1024
        ),
        cost_estimate=pl.CostEstimate(
            flops=flops, bytes_accessed=16 * 1024 * 1024, transcendentals=slots * hidden_units
        ),
    )(
        grad_out,
        routes.T,
        gates.T,
        saved_gate.reshape(slots, hidden_units),
        saved_up.reshape(slots, hidden_units),
        w_down[0],
    )

    results = (grad_gate, grad_up, grad_w, back)
    grad_gate, grad_up, grad_w, back = pl.pallas_call(
        hand_over,
        out_shape=tuple(jax.ShapeDtypeStruct(a.shape, a.dtype) for a in results),
        in_specs=[vmem, vmem, vmem, vmem],
        out_specs=(hbm, hbm, hbm, vmem),
        scratch_shapes=[dma((3, PARTS))],
        compiler_params=pltpu.CompilerParams(vmem_limit_bytes=16 * 1024 * 1024),
    )(*results)
    return (
        grad_gate.reshape(saved_gate.shape),
        grad_up.reshape(saved_up.shape),
        grad_w[None],
        back.T,
    )


def solution(mesh):
    in_specs = (
        P("ep", "tp"),
        P("ep", None),
        P("ep", None),
        P("ep", None, None, "tp"),
        P("ep", None, None, "tp"),
        P("ep", "tp", None),
    )
    out_specs = (
        P("ep", None, None, "tp"),
        P("ep", None, None, "tp"),
        P("ep", "tp", None),
        P("ep", None),
    )
    return jax.shard_map(body, mesh=mesh, in_specs=in_specs, out_specs=out_specs, check_vma=False)
```
